512 devices in a mesh: ctx: 64 (over y, x, z_hi, core), head: 8 (over z_lo).
Axes of the slice: x: 4, y: 4, z: 16 (z_hi: 2, z_lo: 8; z = z_hi * 8 + z_lo), core: 2. Of those that a mesh axis runs over, the one named last changes fastest.
Arguments:
- layer_input: bfloat16 [8192, 2048], P('ctx'), may hold values from -34 to 34
- queries: bfloat16 [8192, 2048], P('ctx', 'head'), may hold values from -30 to 30
- keys: bfloat16 [8192, 2048], P('ctx', 'head'), may hold values from -6 to 6
- values: bfloat16 [8192, 2048], P('ctx', 'head'), may hold values from -6 to 6
- out_weight: bfloat16 [2048, 2048], P('head', 'ctx'), may hold values from -0.125 to 0.125
- out_grad: bfloat16 [8192, 2048], P('ctx'), may hold values from -34 to 34
- query_limits: float32 [4], replicated, may hold values from 0.01 to 0.5
- output_limits: float32 [4], replicated, may hold values from 0.01 to 0.5
Outputs:
- grad_wq: float32 [2048, 2048], P('ctx', 'head')
- grad_wo: float32 [2048, 2048], P('head', 'ctx')
The draws below stay inside these ranges and needn't reach their ends.
All inputs are finite; a program needn't handle non-finite values.
Results may differ from the reference program's by a relative error of at most 0.035.
Values may be sent and summed in bfloat16 or wider, within the bound.
No kernel may reach another device: no remote copies, remote signals or barrier semaphores. Data moves between devices by JAX's collectives and lax.ppermute only.
A program may use at most 64 MiB of HBM per device.

```python
import math
import jax
import jax.numpy as jnp
from jax import lax

D = 2048
HEADS = 16
HD = 128
TOKENS = 8192
QBLK = 4
OBLK = 4


def rising_columns(key, rise):
    position = jnp.arange(D, dtype=jnp.float32) / (D - 1)
    rough = jax.random.uniform(jax.random.fold_in(key, 7), (1, D), jnp.float32, 0.7, 1.4)
    return rough * jnp.exp(position * jnp.log(rise))[None, :]


def draw_queries(key, part):
    key = jax.random.fold_in(key, 1)
    full = jnp.clip(jax.random.normal(key, (TOKENS // 2, 2, HEADS * HD), jnp.float32), -6.0, 6.0)
    return full.reshape(TOKENS, HEADS * HD).astype(jnp.bfloat16)


def draw_keys(key, part):
    key = jax.random.fold_in(key, 2)
    full = jnp.clip(jax.random.normal(key, (TOKENS // 2, 2, HEADS * HD), jnp.float32), -6.0, 6.0)
    return full.reshape(TOKENS, HEADS * HD).astype(jnp.bfloat16)


def draw_layer_input(key, part):
    key = jax.random.fold_in(key, 3)
    base = jnp.clip(jax.random.normal(key, (TOKENS, D), jnp.float32), -6.0, 6.0)
    full = base * rising_columns(key, 4.0)
    return full.astype(jnp.bfloat16)


def draw_out_grad(key, part):
    key = jax.random.fold_in(key, 4)
    base = jnp.clip(jax.random.normal(key, (TOKENS, D), jnp.float32), -6.0, 6.0)
    full = base * rising_columns(key, 4.0)
    return full.astype(jnp.bfloat16)


def level_of(stream_key, dims, cuts, least, high):
    gain, own = 1.0, jax.random.fold_in(stream_key, 6)
    for dim, shards_of in cuts:
        heights = jnp.exp(jax.random.uniform(jax.random.fold_in(own, dim), (shards_of,), jnp.float32, least / len(cuts), high / len(cuts)))
        gain = gain * jnp.repeat(heights, dims[dim] // shards_of).reshape([-1 if axis == dim else 1 for axis in range(len(dims))])
    return gain


def noise(key, dims, scale, bound, shards=(), kind=jnp.bfloat16):
    drawn = scale * jax.random.normal(key, dims, jnp.float32)
    if shards:
        drawn = drawn * level_of(key, dims, shards, -0.22, 0.18)
    return jnp.clip(drawn, -bound, bound).astype(kind)


def setup_inputs(seed: int = 0) -> dict:
    streams_of = jax.random.split(jax.random.key(seed), 9)
    return {
        "layer_input": draw_layer_input(jax.random.fold_in(streams_of[8], 71), 0),
        "queries": draw_queries(jax.random.fold_in(streams_of[8], 71), 0),
        "keys": draw_keys(jax.random.fold_in(streams_of[8], 71), 0),
        "values": noise(streams_of[3], (TOKENS, HEADS * HD), 1.0, 6.0, ((0, 64), (1, 8))),
        "out_weight": noise(streams_of[4], (HEADS * HD, D), (HEADS * HD) ** -0.5, 0.125, ((0, 8), (1, 64))),
        "out_grad": draw_out_grad(jax.random.fold_in(streams_of[8], 71), 0),
        "query_limits": jnp.clip(jnp.exp(jax.random.uniform(streams_of[6], (QBLK,), jnp.float32, math.log(0.01), math.log(0.5))), 0.01, 0.5),
        "output_limits": jnp.clip(jnp.exp(jax.random.uniform(streams_of[7], (OBLK,), jnp.float32, math.log(0.01), math.log(0.5))), 0.01, 0.5),
    }


def widen(array):
    return lax.optimization_barrier(array).astype(jnp.float32)

def clip_rows(raw, limits):
    blocks = raw.reshape(limits.shape[0], -1)
    spread = jnp.sqrt(lax.optimization_barrier(jnp.mean(blocks * blocks, axis=-1)) + 1e-06)
    factor = jnp.minimum(1.0, limits / spread)
    return (blocks * factor[:, None]).reshape(raw.shape)

def reference(layer_input, queries, keys, values, out_weight, out_grad, query_limits, output_limits):
    scale = 1.0 / math.sqrt(HD)
    d_attn = jnp.dot(out_grad, out_weight.T, preferred_element_type=jnp.float32).astype(jnp.bfloat16)
    span = min(512, TOKENS)
    attn_parts = []
    grad_parts = []
    for block in range(TOKENS // span):
        low = block * span
        high = low + span
        q_block = queries[low:high].astype(jnp.float32).reshape(span, HEADS, HD)
        k_block = keys[:high].astype(jnp.float32).reshape(high, HEADS, HD)
        v_block = values[:high].astype(jnp.float32).reshape(high, HEADS, HD)
        scores = jnp.einsum('qhe,khe->hqk', q_block, k_block) * scale
        visible = jnp.arange(high, dtype=jnp.int32)[None, :] <= (low + jnp.arange(span, dtype=jnp.int32))[:, None]
        scores = jnp.where(visible[None], scores, -jnp.inf)
        top = lax.optimization_barrier(jnp.max(scores, axis=-1, keepdims=True))
        lse = top + jnp.log(lax.optimization_barrier(jnp.sum(jnp.exp(scores - top), axis=-1, keepdims=True)))
        probs = jnp.exp(scores - lse)
        probs_low = widen(probs.astype(jnp.bfloat16))
        attn_block = jnp.einsum('hqk,khe->qhe', probs_low, v_block).astype(jnp.bfloat16)
        grad_block = widen(d_attn[low:high]).reshape(span, HEADS, HD)
        delta = lax.optimization_barrier(jnp.sum(grad_block * widen(attn_block), axis=-1))
        d_probs = jnp.einsum('qhe,khe->hqk', grad_block, v_block)
        d_scores = probs * (d_probs - delta.T[:, :, None])
        d_low = widen(d_scores.astype(jnp.bfloat16))
        d_query = (jnp.einsum('hqk,khe->qhe', d_low, k_block) * scale).astype(jnp.bfloat16)
        attn_parts.append(attn_block.reshape(span, HEADS * HD))
        grad_parts.append(d_query.reshape(span, HEADS * HD))
    attn = jnp.concatenate(attn_parts, axis=0)
    d_query = jnp.concatenate(grad_parts, axis=0)
    raw_q = jnp.dot(layer_input.T, d_query, preferred_element_type=jnp.float32)
    raw_o = jnp.dot(attn.T, out_grad, preferred_element_type=jnp.float32)
    return (clip_rows(raw_q, query_limits), clip_rows(raw_o, output_limits))
```

```python
import math

import jax
import jax.numpy as jnp
from jax import lax
from jax.experimental import pallas as pl
from jax.experimental.pallas import tpu as pltpu
from jax.sharding import Mesh, PartitionSpec as P

D = 2048
HD = 128
BLOCK_ROWS = 512
SCALE = 1.0 / math.sqrt(HD)
CTX = ("y", "x", "zh", "core")
PLANE = ("y", "x")
BF = jnp.bfloat16
F32 = jnp.float32


def dot(left, right, dims):
    return lax.dot_general(left, right, (dims, ((), ())), preferred_element_type=F32)


def fold(x, op):
    return op(x[:, :HD], x[:, HD:])


def attention_kernel(place, q_ref, g_ref, mine_ref, peer_ref, o_ref, dq_ref, s_ref):
    last, half, core = place[0], place[1], place[2]
    q = q_ref[...]
    g = g_ref[...]
    rows = q.shape[0]
    sources = (mine_ref, peer_ref)

    def keys(i, t):
        return sources[t][i, 0:256, :]

    def values(i, t):
        return sources[t][i, 256:512, :]

    def scores(i, top, masked):
        for t in range(2):
            s = dot(q, keys(i, t), ((1,), (1,)))
            if masked:
                r = lax.broadcasted_iota(jnp.int32, s.shape, 0)
                c = lax.broadcasted_iota(jnp.int32, s.shape, 1)
                own = r < HD
                q_pos = half * 256 + jnp.where(own, core * HD + r, (1 - core) * HD + r - HD)
                k_pos = (half if t == 0 else 1 - half) * 256 + c
                s = jnp.where(k_pos <= q_pos, s, -jnp.inf)
            s_ref[i, t] = s
            top = jnp.maximum(top, fold(s, jnp.maximum))
        return top

    top = jnp.full((rows, HD), -jnp.inf, F32)
    top = lax.fori_loop(0, last, lambda i, top: scores(i, top, False), top)
    top = scores(last, top, True)
    top = jnp.max(top, axis=1, keepdims=True)

    def forward(i, carry):
        total, out = carry
        for t in range(2):
            e = jnp.exp((s_ref[i, t] - top) * SCALE)
            s_ref[i, t] = e
            total = total + fold(e, jnp.add)
            out = out + dot(e.astype(BF), values(i, t), ((1,), (0,)))
        return total, out

    zero = jnp.zeros((rows, HD), F32)
    total, out = lax.fori_loop(0, last + 1, forward, (zero, zero))
    inverse = 1.0 / jnp.sum(total, axis=1, keepdims=True)
    attn = (out * inverse).astype(BF)
    o_ref[...] = attn
    delta = jnp.sum(g.astype(F32) * attn.astype(F32), axis=1, keepdims=True)

    def backward(i, grad):
        for t in range(2):
            dp = dot(g, values(i, t), ((1,), (1,)))
            ds = s_ref[i, t] * (dp - delta)
            grad = grad + dot(ds.astype(BF), keys(i, t), ((1,), (0,)))
        return grad

    grad = lax.fori_loop(0, last + 1, backward, zero)
    dq_ref[...] = (grad * (inverse * SCALE)).astype(BF)


def attention(place, q, g, mine, peer):
    blocks = mine.shape[0]
    rows = q.shape[0]
    whole = pl.BlockSpec(memory_space=pltpu.VMEM)
    out = jax.ShapeDtypeStruct(q.shape, BF)
    return pl.pallas_call(
        attention_kernel,
        out_shape=(out, out),
        in_specs=[pl.BlockSpec(memory_space=pltpu.SMEM)] + [whole] * 4,
        out_specs=(whole, whole),
        scratch_shapes=[pltpu.VMEM((blocks, 2, rows, 256), F32)],
        compiler_params=pltpu.CompilerParams(vmem_limit_bytes=48 * 2**20),
    )(place, q, g, mine, peer)


def swap(x, axis):
    return lax.ppermute(x, axis, [(0, 1), (1, 0)])


def spread(x, axes, n):
    return lax.all_to_all(
        jnp.broadcast_to(x[None], (n,) + x.shape), axes, split_axis=0, concat_axis=0, tiled=True
    )


def shards(layer_input, queries, keys, values, out_weight, out_grad, query_limits, output_limits):
    y, x, half, core, head = (lax.axis_index(a) for a in CTX + ("head",))
    first = core == 0

    def split(a):
        low, high = a[:, :HD], a[:, HD:]
        return jnp.where(first, low, high), jnp.where(first, high, low)

    pairs = [split(a) for a in (keys, values, out_weight.T, queries)]
    kept = jnp.concatenate([own for own, _ in pairs], axis=0)
    got = swap(jnp.concatenate([other for _, other in pairs], axis=0), "core")
    n = keys.shape[0]
    cols = out_weight.shape[1]
    low, high = jnp.where(first, kept, got), jnp.where(first, got, kept)
    k2 = jnp.concatenate([low[:n], high[:n]], axis=0)
    v2 = jnp.concatenate([low[n : 2 * n], high[n : 2 * n]], axis=0)
    w2 = jnp.concatenate([low[2 * n : 2 * n + cols], high[2 * n : 2 * n + cols]], axis=0)
    mine = jnp.concatenate([k2, v2, w2], axis=0)
    q2 = jnp.concatenate([kept[2 * n + cols :], got[2 * n + cols :]], axis=0)

    peer = swap(mine, "zh")
    all_mine = spread(mine, PLANE, 16)
    all_peer = spread(peer, PLANE, 16)

    g2 = jnp.concatenate([out_grad, swap(out_grad, "core")], axis=0)
    x2 = jnp.concatenate([layer_input, swap(layer_input, "core")], axis=0)

    wm, wp = all_mine[:, 4 * n :], all_peer[:, 4 * n :]
    near = half == 0
    weight = jnp.stack([jnp.where(near, wm, wp), jnp.where(near, wp, wm)], axis=1).reshape(D, HD)
    d_attn = dot(g2, weight, ((1,), (0,))).astype(BF)

    place = jnp.stack([y * 4 + x, half, core]).astype(jnp.int32)
    attn, d_query = attention(place, q2, d_attn, all_mine, all_peer)

    part_q = dot(x2, d_query, ((0,), (0,))).astype(BF).reshape(16, D // 16, HD)
    part_o = dot(g2, attn, ((0,), (0,))).astype(BF).reshape(16, D // 16, HD)
    parts = lax.all_to_all(
        jnp.concatenate([part_q, part_o], axis=1), PLANE, split_axis=0, concat_axis=0, tiled=True
    )
    summed = jnp.sum(parts.astype(F32), axis=0)
    pieces = summed.reshape(2, 4, 32, HD).transpose(1, 0, 2, 3)
    pieces = lax.all_to_all(pieces, ("zh", "core"), split_axis=0, concat_axis=0, tiled=True)
    pieces = pieces.reshape(2, 2, 2, 32, HD)
    raw = pieces[0] + pieces[1]
    raw_q = jnp.concatenate([raw[0, 0], raw[1, 0]], axis=1)
    raw_o = jnp.concatenate([raw[0, 1], raw[1, 1]], axis=1)

    lane = lax.broadcasted_iota(jnp.int32, (1, 128), 1)
    sums = jnp.where(lane == y, jnp.sum(raw_q * raw_q), 0.0) + jnp.where(
        lane == 4 + head // 2, jnp.sum(raw_o * raw_o), 0.0
    )
    sums = jnp.sum(spread(sums, ("y", "x", "core"), 32), axis=0)
    sums = jnp.sum(spread(sums, ("zh", "head"), 16), axis=0)

    def factor(total, limits, block):
        spread_of = jnp.sqrt(total / (BLOCK_ROWS * D) + 1e-06)
        every = jnp.minimum(1.0, limits / spread_of)
        return jnp.sum(jnp.where(jnp.arange(4) == block, every, 0.0))

    grad_wq = raw_q * factor(sums[0, 0:4], query_limits, y)
    grad_wo = (raw_o * factor(sums[0, 4:8], output_limits, head // 2)).T
    return (grad_wq, grad_wo)


def solution(mesh):
    fine = Mesh(mesh.devices.reshape(4, 4, 2, 2, 8), CTX + ("head",))
    in_specs = (
        P(CTX, None),
        P(CTX, "head"),
        P(CTX, "head"),
        P(CTX, "head"),
        P("head", CTX),
        P(CTX, None),
        P(),
        P(),
    )
    out_specs = (P(CTX, "head"), P("head", CTX))
    return jax.shard_map(shards, mesh=fine, in_specs=in_specs, out_specs=out_specs, check_vma=False)
```

```python
import math

import jax
import jax.numpy as jnp
from jax import lax
from jax.experimental import pallas as pl
from jax.experimental.pallas import tpu as pltpu
from jax.sharding import Mesh, PartitionSpec as P

D = 2048
HD = 128
BLOCK_ROWS = 512
SCALE = 1.0 / math.sqrt(HD)
CTX = ("y", "x", "zh", "core")
PLANE = ("y", "x")
BF = jnp.bfloat16
F32 = jnp.float32


def dot(left, right, dims):
    return lax.dot_general(left, right, (dims, ((), ())), preferred_element_type=F32)


def fold(x, op):
    return op(x[:, :HD], x[:, HD:])


def attention_kernel(place, q_ref, g_ref, mine_ref, peer_ref, o_ref, dq_ref, s_ref):
    last, half, core = place[0], place[1], place[2]
    q = q_ref[...]
    g = g_ref[...]
    rows = q.shape[0]
    steps = [(i, t) for i in range(mine_ref.shape[0]) for t in range(2)]
    sources = (mine_ref, peer_ref)

    def keys(i, t):
        return sources[t][i, 0:256, :]

    def values(i, t):
        return sources[t][i, 256:512, :]

    r = lax.broadcasted_iota(jnp.int32, (rows, 256), 0)
    c = lax.broadcasted_iota(jnp.int32, (rows, 256), 1)
    q_pos = half * 256 + jnp.where(r < HD, core * HD + r, (1 - core) * HD + r - HD)
    ahead = [(half if t == 0 else 1 - half) * 256 + c - q_pos for t in range(2)]

    top = jnp.full((rows, HD), -jnp.inf, F32)
    for i, t in steps:
        s = dot(q, keys(i, t), ((1,), (1,)))
        s = jnp.where(ahead[t] <= (last - i) * 512, s, -jnp.inf)
        s_ref[i, t] = s
        top = jnp.maximum(top, fold(s, jnp.maximum))
    top = jnp.max(top, axis=1, keepdims=True)

    total = jnp.zeros((rows, HD), F32)
    out = jnp.zeros((rows, HD), F32)
    for i, t in steps:
        e = jnp.exp((s_ref[i, t] - top) * SCALE)
        s_ref[i, t] = e
        total = total + fold(e, jnp.add)
        out = out + dot(e.astype(BF), values(i, t), ((1,), (0,)))
    inverse = 1.0 / jnp.sum(total, axis=1, keepdims=True)
    attn = (out * inverse).astype(BF)
    o_ref[...] = attn
    delta = jnp.sum(g.astype(F32) * attn.astype(F32), axis=1, keepdims=True)

    grad = jnp.zeros((rows, HD), F32)
    for i, t in steps:
        dp = dot(g, values(i, t), ((1,), (1,)))
        ds = s_ref[i, t] * (dp - delta)
        grad = grad + dot(ds.astype(BF), keys(i, t), ((1,), (0,)))
    dq_ref[...] = (grad * (inverse * SCALE)).astype(BF)


def attention(place, q, g, mine, peer):
    blocks = mine.shape[0]
    rows = q.shape[0]
    whole = pl.BlockSpec(memory_space=pltpu.VMEM)
    out = jax.ShapeDtypeStruct(q.shape, BF)
    return pl.pallas_call(
        attention_kernel,
        out_shape=(out, out),
        in_specs=[pl.BlockSpec(memory_space=pltpu.SMEM)] + [whole] * 4,
        out_specs=(whole, whole),
        scratch_shapes=[pltpu.VMEM((blocks, 2, rows, 256), F32)],
        compiler_params=pltpu.CompilerParams(vmem_limit_bytes=48 * 2**20),
    )(place, q, g, mine, peer)


def swap(x, axis):
    return lax.ppermute(x, axis, [(0, 1), (1, 0)])


def spread(x, axes, n):
    return lax.all_to_all(
        jnp.broadcast_to(x[None], (n,) + x.shape), axes, split_axis=0, concat_axis=0, tiled=True
    )


def shards(layer_input, queries, keys, values, out_weight, out_grad, query_limits, output_limits):
    y, x, half, core, head = (lax.axis_index(a) for a in CTX + ("head",))
    first = core == 0

    def split(a):
        low, high = a[:, :HD], a[:, HD:]
        return jnp.where(first, low, high), jnp.where(first, high, low)

    pairs = [split(a) for a in (keys, values, out_weight.T, queries)]
    kept = jnp.concatenate([own for own, _ in pairs], axis=0)
    got = swap(jnp.concatenate([other for _, other in pairs], axis=0), "core")
    n = keys.shape[0]
    cols = out_weight.shape[1]
    low, high = jnp.where(first, kept, got), jnp.where(first, got, kept)
    k2 = jnp.concatenate([low[:n], high[:n]], axis=0)
    v2 = jnp.concatenate([low[n : 2 * n], high[n : 2 * n]], axis=0)
    w2 = jnp.concatenate([low[2 * n : 2 * n + cols], high[2 * n : 2 * n + cols]], axis=0)
    mine = jnp.concatenate([k2, v2, w2], axis=0)
    q2 = jnp.concatenate([kept[2 * n + cols :], got[2 * n + cols :]], axis=0)

    peer = swap(mine, "zh")
    all_mine = spread(mine, PLANE, 16)
    all_peer = spread(peer, PLANE, 16)

    g2 = jnp.concatenate([out_grad, swap(out_grad, "core")], axis=0)
    x2 = jnp.concatenate([layer_input, swap(layer_input, "core")], axis=0)

    wm, wp = all_mine[:, 4 * n :], all_peer[:, 4 * n :]
    near = half == 0
    weight = jnp.stack([jnp.where(near, wm, wp), jnp.where(near, wp, wm)], axis=1).reshape(D, HD)
    d_attn = dot(g2, weight, ((1,), (0,))).astype(BF)

    place = jnp.stack([y * 4 + x, half, core]).astype(jnp.int32)
    attn, d_query = attention(place, q2, d_attn, all_mine, all_peer)

    part_q = dot(x2, d_query, ((0,), (0,))).astype(BF).reshape(16, D // 16, HD)
    part_o = dot(g2, attn, ((0,), (0,))).astype(BF).reshape(16, D // 16, HD)
    parts = lax.all_to_all(
        jnp.concatenate([part_q, part_o], axis=1), PLANE, split_axis=0, concat_axis=0, tiled=True
    )
    summed = jnp.sum(parts.astype(F32), axis=0)
    raw = summed + swap(summed, "zh")

    rows = D // 16
    lane = lax.broadcasted_iota(jnp.int32, (1, 128), 1)
    sums = jnp.where(lane == y, jnp.sum(raw[:rows] * raw[:rows]), 0.0) + jnp.where(
        lane == 4 + head // 2, jnp.sum(raw[rows:] * raw[rows:]), 0.0
    )
    sums = jnp.sum(spread(sums, ("y", "x", "core", "head"), 256), axis=0)

    def piece(which, of_core):
        return lax.dynamic_slice_in_dim(raw, which * rows + (half * 2 + of_core) * 32, 32, axis=0)

    given = swap(jnp.concatenate([piece(0, 1 - core), piece(1, 1 - core)], axis=0), "core")
    own_q, own_o = piece(0, core), piece(1, core)

    def join(own, other):
        return jnp.concatenate([jnp.where(first, own, other), jnp.where(first, other, own)], axis=1)

    raw_q = join(own_q, given[:32])
    raw_o = join(own_o, given[32:]).T

    def factor(total, limits, block):
        every = jnp.minimum(1.0, limits / jnp.sqrt(total / (BLOCK_ROWS * D) + 1e-06))
        return jnp.sum(jnp.where(jnp.arange(4) == block, every, 0.0))

    grad_wq = raw_q * factor(sums[0, 0:4], query_limits, y)
    grad_wo = raw_o * factor(sums[0, 4:8], output_limits, head // 2)
    return (grad_wq, grad_wo)


def solution(mesh):
    fine = Mesh(mesh.devices.reshape(4, 4, 2, 2, 8), CTX + ("head",))
    in_specs = (
        P(CTX, None),
        P(CTX, "head"),
        P(CTX, "head"),
        P(CTX, "head"),
        P("head", CTX),
        P(CTX, None),
        P(),
        P(),
    )
    out_specs = (P(CTX, "head"), P("head", CTX))
    return jax.shard_map(shards, mesh=fine, in_specs=in_specs, out_specs=out_specs, check_vma=False)
```

```python
import math

import jax
import jax.numpy as jnp
from jax import lax
from jax.experimental import pallas as pl
from jax.experimental.pallas import tpu as pltpu
from jax.sharding import Mesh, PartitionSpec as P

D = 2048
HD = 128
BLOCK_ROWS = 512
SCALE = 1.0 / math.sqrt(HD)
CTX = ("y", "x", "zh", "core")
PLANE = ("y", "x")
BF = jnp.bfloat16
F32 = jnp.float32


def dot(left, right, dims):
    return lax.dot_general(left, right, (dims, ((), ())), preferred_element_type=F32)


def fold(x, op):
    return op(x[:, :HD], x[:, HD:])


def attention_kernel(place, q_ref, g_ref, x_ref, mine_ref, peer_ref, part_ref, s_ref):
    last, half = place[0], place[1]
    q = q_ref[...]
    rows = q.shape[0]
    chips = peer_ref.shape[0]
    steps = [(i, t) for i in range(chips) for t in range(2)]

    sources = (mine_ref, peer_ref)

    def pair(i, t, start, size):
        cuts = [slice(core * 288 + start, core * 288 + start + size) for core in range(2)]
        return jnp.concatenate([sources[t][i, cut, :] for cut in cuts], axis=0)

    def keys(i, t):
        return pair(i, t, 0, 128)

    def values(i, t):
        return pair(i, t, 128, 128)

    r = lax.broadcasted_iota(jnp.int32, (rows, 256), 0)
    c = lax.broadcasted_iota(jnp.int32, (rows, 256), 1)
    ahead = [c - r, c - r + (1 - 2 * half) * 256]

    top = jnp.full((rows, HD), -jnp.inf, F32)
    for i, t in steps:
        s = dot(q, keys(i, t), ((1,), (1,)))
        s = jnp.where(ahead[t] <= (last - i) * 512, s, -jnp.inf)
        s_ref[i, t] = s
        top = jnp.maximum(top, fold(s, jnp.maximum))
    top = jnp.max(top, axis=1, keepdims=True)

    g = jnp.zeros((rows, HD), F32)
    for i in range(chips):
        near, far = pair(i, 0, 256, 32), pair(i, 1, 256, 32)
        weight = jnp.concatenate(
            [jnp.where(half == 0, near, far), jnp.where(half == 0, far, near)], axis=0
        )
        g = g + dot(g_ref[:, i * HD : (i + 1) * HD], weight, ((1,), (0,)))
    g = g.astype(BF)

    total = jnp.zeros((rows, HD), F32)
    out = jnp.zeros((rows, HD), F32)
    for i, t in steps:
        e = jnp.exp((s_ref[i, t] - top) * SCALE)
        s_ref[i, t] = e
        total = total + fold(e, jnp.add)
        out = out + dot(e.astype(BF), values(i, t), ((1,), (0,)))
    inverse = 1.0 / jnp.sum(total, axis=1, keepdims=True)
    attn = (out * inverse).astype(BF)
    delta = jnp.sum(g.astype(F32) * attn.astype(F32), axis=1, keepdims=True)

    grad = jnp.zeros((rows, HD), F32)
    for i, t in steps:
        dp = dot(g, values(i, t), ((1,), (1,)))
        ds = s_ref[i, t] * (dp - delta)
        grad = grad + dot(ds.astype(BF), keys(i, t), ((1,), (0,)))
    grad = (grad * (inverse * SCALE)).astype(BF)

    for i in range(chips):
        cut = slice(i * HD, (i + 1) * HD)
        part_ref[i, 0:HD, :] = dot(x_ref[:, cut], grad, ((0,), (0,))).astype(BF)
        part_ref[i, HD : 2 * HD, :] = dot(g_ref[:, cut], attn, ((0,), (0,))).astype(BF)


def attention(place, q, g, x, mine, peer):
    rows = q.shape[0]
    chips = peer.shape[0]
    whole = pl.BlockSpec(memory_space=pltpu.VMEM)
    return pl.pallas_call(
        attention_kernel,
        out_shape=jax.ShapeDtypeStruct((chips, 2 * HD, HD), BF),
        in_specs=[pl.BlockSpec(memory_space=pltpu.SMEM)] + [whole] * 5,
        out_specs=whole,
        scratch_shapes=[pltpu.VMEM((chips, 2, rows, 256), F32)],
        compiler_params=pltpu.CompilerParams(vmem_limit_bytes=48 * 2**20),
    )(place, q, g, x, mine, peer)


def swap(x, axis):
    return lax.ppermute(x, axis, [(0, 1), (1, 0)])


def spread(x, axes, n):
    return lax.all_to_all(
        jnp.broadcast_to(x[None], (n,) + x.shape), axes, split_axis=0, concat_axis=0, tiled=True
    )


def shards(layer_input, queries, keys, values, out_weight, out_grad, query_limits, output_limits):
    y, x, half, core, head = (lax.axis_index(a) for a in CTX + ("head",))
    first = core == 0

    n, cols = keys.shape[0], out_weight.shape[1]
    block = jnp.concatenate([keys, values, out_weight.T, queries], axis=0)
    block = jnp.stack([block[:, :HD], block[:, HD:]], axis=0)
    block = lax.all_to_all(block, "core", split_axis=0, concat_axis=0, tiled=True)
    q2 = block[:, 2 * n + cols :].reshape(2 * n, HD)

    mine = block[:, : 2 * n + cols].reshape(2 * (2 * n + cols), HD)
    all_mine = spread(mine, PLANE, 16)
    all_peer = spread(swap(mine, "zh"), PLANE, 16)

    def both(a):
        other = swap(a, "core")
        return jnp.concatenate([jnp.where(first, a, other), jnp.where(first, other, a)], axis=0)

    g2, x2 = both(out_grad), both(layer_input)
    place = jnp.stack([y * 4 + x, half]).astype(jnp.int32)
    parts = attention(place, q2, g2, x2, all_mine, all_peer)
    parts = lax.all_to_all(parts, PLANE, split_axis=0, concat_axis=0, tiled=True)
    summed = jnp.sum(parts.astype(F32), axis=0)
    raw = summed + swap(summed.astype(BF), "zh").astype(F32)

    rows = D // 16
    lane = lax.broadcasted_iota(jnp.int32, (1, 128), 1)
    sums = jnp.where(lane == y, jnp.sum(raw[:rows] * raw[:rows]), 0.0) + jnp.where(
        lane == 4 + head // 2, jnp.sum(raw[rows:] * raw[rows:]), 0.0
    )
    sums = jnp.sum(spread(sums, PLANE, 16), axis=0)
    sums = jnp.sum(spread(sums, ("core", "head"), 16), axis=0)

    def piece(which, of_core):
        return lax.dynamic_slice_in_dim(raw, which * rows + (half * 2 + of_core) * 32, 32, axis=0)

    given = swap(jnp.concatenate([piece(0, 1 - core), piece(1, 1 - core)], axis=0), "core")
    own_q, own_o = piece(0, core), piece(1, core)

    def join(own, other):
        return jnp.concatenate([jnp.where(first, own, other), jnp.where(first, other, own)], axis=1)

    raw_q = join(own_q, given[:32])
    raw_o = join(own_o, given[32:]).T

    def factor(total, limits, block):
        every = jnp.minimum(1.0, limits / jnp.sqrt(total / (BLOCK_ROWS * D) + 1e-06))
        return jnp.sum(jnp.where(jnp.arange(4) == block, every, 0.0))

    grad_wq = raw_q * factor(sums[0, 0:4], query_limits, y)
    grad_wo = raw_o * factor(sums[0, 4:8], output_limits, head // 2)
    return (grad_wq, grad_wo)


def solution(mesh):
    fine = Mesh(mesh.devices.reshape(4, 4, 2, 2, 8), CTX + ("head",))
    in_specs = (
        P(CTX, None),
        P(CTX, "head"),
        P(CTX, "head"),
        P(CTX, "head"),
        P("head", CTX),
        P(CTX, None),
        P(),
        P(),
    )
    out_specs = (P(CTX, "head"), P("head", CTX))
    return jax.shard_map(shards, mesh=fine, in_specs=in_specs, out_specs=out_specs, check_vma=False)
```

```python
import math

import jax
import jax.numpy as jnp
from jax import lax
from jax.experimental import pallas as pl
from jax.experimental.pallas import tpu as pltpu
from jax.sharding import Mesh, PartitionSpec as P

D = 2048
HD = 128
BLOCK_ROWS = 512
SCALE = 1.0 / math.sqrt(HD)
SCALE_LOG2E = SCALE * math.log2(math.e)
CTX = ("y", "x", "zh", "core")
PLANE = ("y", "x")
BF = jnp.bfloat16
F32 = jnp.float32


def dot(left, right, dims):
    return lax.dot_general(left, right, (dims, ((), ())), preferred_element_type=F32)


def fold(x, op):
    return op(x[:, :HD], x[:, HD:])


def attention_kernel(place, q_ref, g_ref, x_ref, mine_ref, peer_ref, part_ref, s_ref):
    last, half = place[0], place[1]
    q = q_ref[...]
    rows = q.shape[0]
    chips = peer_ref.shape[0]
    steps = [(i, t) for i in range(chips) for t in range(2)]

    sources = (mine_ref, peer_ref)

    def pair(i, t, start, size):
        cuts = [slice(core * 288 + start, core * 288 + start + size) for core in range(2)]
        return jnp.concatenate([sources[t][i, cut, :] for cut in cuts], axis=0)

    def keys(i, t):
        return pair(i, t, 0, 128)

    def values(i, t):
        return pair(i, t, 128, 128)

    r = lax.broadcasted_iota(jnp.int32, (rows, 256), 0)
    c = lax.broadcasted_iota(jnp.int32, (rows, 256), 1)
    ahead = [c - r, c - r + (1 - 2 * half) * 256]

    top = jnp.full((rows, HD), -jnp.inf, F32)
    for i, t in steps:
        s = dot(q, keys(i, t), ((1,), (1,)))
        s = jnp.where(ahead[t] <= (last - i) * 512, s, -jnp.inf)
        s_ref[i, t] = s
        top = jnp.maximum(top, fold(s, jnp.maximum))
    top = jnp.max(top, axis=1, keepdims=True)

    g = jnp.zeros((rows, HD), F32)
    for i in range(chips):
        near, far = pair(i, 0, 256, 32), pair(i, 1, 256, 32)
        weight = jnp.concatenate(
            [jnp.where(half == 0, near, far), jnp.where(half == 0, far, near)], axis=0
        )
        g = g + dot(g_ref[:, i * HD : (i + 1) * HD], weight, ((1,), (0,)))
    g = g.astype(BF)

    total = jnp.zeros((rows, HD), F32)
    out = jnp.zeros((rows, HD), F32)
    for i, t in steps:
        e = jnp.exp2((s_ref[i, t] - top) * SCALE_LOG2E)
        s_ref[i, t] = e
        total = total + fold(e, jnp.add)
        out = out + dot(e.astype(BF), values(i, t), ((1,), (0,)))
    inverse = 1.0 / jnp.sum(total, axis=1, keepdims=True)
    attn = (out * inverse).astype(BF)
    delta = jnp.sum(g.astype(F32) * attn.astype(F32), axis=1, keepdims=True)

    grad = jnp.zeros((rows, HD), F32)
    for i, t in steps:
        dp = dot(g, values(i, t), ((1,), (1,)))
        ds = s_ref[i, t] * (dp - delta)
        grad = grad + dot(ds.astype(BF), keys(i, t), ((1,), (0,)))
    grad = (grad * (inverse * SCALE)).astype(BF)

    for i in range(chips):
        cut = slice(i * HD, (i + 1) * HD)
        for n, (left, right) in enumerate(((x_ref, grad), (g_ref, attn))):
            part = dot(left[:, cut], right, ((0,), (0,))).astype(BF)
            for m in range(4):
                half_of, core_of = m // 2, m % 2
                to = n * 64 + half_of * 32
                part_ref[2 * i + core_of, to : to + 32, :] = part[m * 32 : m * 32 + 32]


def attention(place, q, g, x, mine, peer):
    rows = q.shape[0]
    chips = peer.shape[0]
    whole = pl.BlockSpec(memory_space=pltpu.VMEM)
    return pl.pallas_call(
        attention_kernel,
        out_shape=jax.ShapeDtypeStruct((2 * chips, HD, HD), BF),
        in_specs=[pl.BlockSpec(memory_space=pltpu.SMEM)] + [whole] * 5,
        out_specs=whole,
        scratch_shapes=[pltpu.VMEM((chips, 2, rows, 256), F32)],
        compiler_params=pltpu.CompilerParams(vmem_limit_bytes=48 * 2**20),
    )(place, q, g, x, mine, peer)


def finished_kernel(place, own_ref, got_ref, q_ref, o_ref, sums_ref):
    raw = own_ref[...] + got_ref[...].astype(F32)
    lane = lax.broadcasted_iota(jnp.int32, (1, 128), 1)
    sums = jnp.zeros((1, 128), F32)
    for n, ref in enumerate((q_ref, o_ref)):
        piece = jnp.concatenate([raw[head, n * 64 : n * 64 + 64] for head in range(2)], axis=1)
        ref[...] = jnp.where(place[2] == 0, piece[:32], piece[32:])
        squares = jnp.sum(jnp.sum(piece * piece, axis=0, keepdims=True), axis=1, keepdims=True)
        sums = sums + jnp.where(lane == place[n], squares, 0.0)
    sums_ref[...] = jnp.broadcast_to(sums[None], sums_ref.shape)


def clip_kernel(place, sums_ref, limits_ref, q_ref, o_ref, grad_q_ref, grad_o_ref):
    total = jnp.sum(sums_ref[...], axis=0)
    every = jnp.minimum(1.0, limits_ref[...] / jnp.sqrt(total / (BLOCK_ROWS * D) + 1e-06))
    lane = lax.broadcasted_iota(jnp.int32, (1, 128), 1)
    for n, (raw_ref, grad_ref) in enumerate(((q_ref, grad_q_ref), (o_ref, grad_o_ref))):
        factor = jnp.sum(jnp.where(lane == place[n], every, 0.0), axis=1, keepdims=True)
        grad_ref[...] = raw_ref[...] * factor


def small_call(kernel, outs, scalars, *arrays):
    whole = pl.BlockSpec(memory_space=pltpu.VMEM)
    return pl.pallas_call(
        kernel,
        out_shape=tuple(jax.ShapeDtypeStruct(shape, F32) for shape in outs),
        in_specs=[pl.BlockSpec(memory_space=pltpu.SMEM)] + [whole] * len(arrays),
        out_specs=(whole,) * len(outs),
    )(scalars, *arrays)


def swap(x, axis):
    return lax.ppermute(x, axis, [(0, 1), (1, 0)])


def spread(x, axes, n):
    return lax.all_to_all(
        jnp.broadcast_to(x[None], (n,) + x.shape), axes, split_axis=0, concat_axis=0, tiled=True
    )


def shards(layer_input, queries, keys, values, out_weight, out_grad, query_limits, output_limits):
    y, x, half, core, head = (lax.axis_index(a) for a in CTX + ("head",))
    first = core == 0

    n, cols = keys.shape[0], out_weight.shape[1]
    block = jnp.concatenate([keys, values, out_weight.T, queries], axis=0)
    block = jnp.stack([block[:, :HD], block[:, HD:]], axis=0)
    block = lax.all_to_all(block, "core", split_axis=0, concat_axis=0, tiled=True)
    q2 = block[:, 2 * n + cols :].reshape(2 * n, HD)

    mine = block[:, : 2 * n + cols].reshape(2 * (2 * n + cols), HD)
    all_mine = spread(mine, PLANE, 16)
    all_peer = spread(swap(mine, "zh"), PLANE, 16)

    def both(a):
        other = swap(a, "core")
        return jnp.concatenate([jnp.where(first, a, other), jnp.where(first, other, a)], axis=0)

    g2, x2 = both(out_grad), both(layer_input)
    place = jnp.stack([y * 4 + x, half]).astype(jnp.int32)
    parts = attention(place, q2, g2, x2, all_mine, all_peer)

    parts = lax.all_to_all(parts, ("y", "x", "core"), split_axis=0, concat_axis=0, tiled=True)
    summed = jnp.sum(parts.astype(F32).reshape(16, 2, HD, HD), axis=0)
    got = swap(summed.astype(BF), "zh")
    place = jnp.stack([y, 4 + head // 2, half]).astype(jnp.int32)
    shape = (D // 64, 2 * HD)
    raw_q, raw_o, sums = small_call(finished_kernel, (shape, shape, (8, 1, 128)), place, summed, got)

    sums = lax.all_to_all(sums, ("x", "core"), split_axis=0, concat_axis=0, tiled=True)
    sums = spread(jnp.sum(sums, axis=0), ("y", "head"), 32)
    limits = jnp.concatenate([query_limits, output_limits, jnp.ones(120, F32)])[None]
    grad_wq, grad_wo = small_call(clip_kernel, (shape, shape), place, sums, limits, raw_q, raw_o)
    return (grad_wq, grad_wo.T)


def solution(mesh):
    fine = Mesh(mesh.devices.reshape(4, 4, 2, 2, 8), CTX + ("head",))
    in_specs = (
        P(CTX, None),
        P(CTX, "head"),
        P(CTX, "head"),
        P(CTX, "head"),
        P("head", CTX),
        P(CTX, None),
        P(),
        P(),
    )
    out_specs = (P(CTX, "head"), P("head", CTX))
    return jax.shard_map(shards, mesh=fine, in_specs=in_specs, out_specs=out_specs, check_vma=False)
```

```python
import math

import jax
import jax.numpy as jnp
from jax import lax
from jax.experimental import pallas as pl
from jax.experimental.pallas import tpu as pltpu
from jax.sharding import Mesh, PartitionSpec as P

D = 2048
HD = 128
BLOCK_ROWS = 512
SCALE = 1.0 / math.sqrt(HD)
SCALE_LOG2E = SCALE * math.log2(math.e)
CTX = ("y", "x", "zh", "core")
PLANE = ("y", "x")
BF = jnp.bfloat16
F32 = jnp.float32


def dot(left, right, dims):
    return lax.dot_general(left, right, (dims, ((), ())), preferred_element_type=F32)


def fold(x, op):
    return op(x[:, :HD], x[:, HD:])


def attention_kernel(place, q_ref, g_ref, x_ref, mine_ref, peer_ref, part_ref, s_ref):
    last, half, core = place[0], place[1], place[2]
    q = q_ref[...]
    rows = q.shape[0]
    chips = peer_ref.shape[0]
    steps = [(i, t) for i in range(chips) for t in range(2)]
    chip = [jnp.where(core == 0, i, i % 4 * 4 + i // 4) for i in range(chips)]

    sources = (mine_ref, peer_ref)

    def pair(i, t, start, size):
        cuts = [slice(core * 288 + start, core * 288 + start + size) for core in range(2)]
        return jnp.concatenate([sources[t][i, cut, :] for cut in cuts], axis=0)

    def keys(i, t):
        return pair(i, t, 0, 128)

    def values(i, t):
        return pair(i, t, 128, 128)

    r = lax.broadcasted_iota(jnp.int32, (rows, 256), 0)
    c = lax.broadcasted_iota(jnp.int32, (rows, 256), 1)
    ahead = [c - r, c - r + (1 - 2 * half) * 256]

    top = jnp.full((rows, HD), -jnp.inf, F32)
    for i, t in steps:
        s = dot(q, keys(i, t), ((1,), (1,)))
        s = jnp.where(ahead[t] <= (last - chip[i]) * 512, s, -jnp.inf)
        s_ref[i, t] = s
        top = jnp.maximum(top, fold(s, jnp.maximum))
    top = jnp.max(top, axis=1, keepdims=True)

    g = jnp.zeros((rows, HD), F32)
    for i in range(chips):
        near, far = pair(i, 0, 256, 32), pair(i, 1, 256, 32)
        weight = jnp.concatenate(
            [jnp.where(half == 0, near, far), jnp.where(half == 0, far, near)], axis=0
        )
        g = g + dot(g_ref[:, pl.ds(pl.multiple_of(chip[i] * HD, HD), HD)], weight, ((1,), (0,)))
    g = g.astype(BF)

    total = jnp.zeros((rows, HD), F32)
    out = jnp.zeros((rows, HD), F32)
    for i, t in steps:
        e = jnp.exp2((s_ref[i, t] - top) * SCALE_LOG2E)
        s_ref[i, t] = e
        total = total + fold(e, jnp.add)
        out = out + dot(e.astype(BF), values(i, t), ((1,), (0,)))
    inverse = 1.0 / jnp.sum(total, axis=1, keepdims=True)
    attn = (out * inverse).astype(BF)
    delta = jnp.sum(g.astype(F32) * attn.astype(F32), axis=1, keepdims=True)

    grad = jnp.zeros((rows, HD), F32)
    for i, t in steps:
        dp = dot(g, values(i, t), ((1,), (1,)))
        ds = s_ref[i, t] * (dp - delta)
        grad = grad + dot(ds.astype(BF), keys(i, t), ((1,), (0,)))
    grad = (grad * (inverse * SCALE)).astype(BF)

    for i in range(chips):
        cut = slice(i * HD, (i + 1) * HD)
        for n, (left, right) in enumerate(((x_ref, grad), (g_ref, attn))):
            part = dot(left[:, cut], right, ((0,), (0,))).astype(BF)
            for m in range(4):
                half_of, core_of = m // 2, m % 2
                to = n * 64 + half_of * 32
                part_ref[2 * i + core_of, to : to + 32, :] = part[m * 32 : m * 32 + 32]


def attention(place, q, g, x, mine, peer):
    rows = q.shape[0]
    chips = peer.shape[0]
    whole = pl.BlockSpec(memory_space=pltpu.VMEM)
    return pl.pallas_call(
        attention_kernel,
        out_shape=jax.ShapeDtypeStruct((2 * chips, HD, HD), BF),
        in_specs=[pl.BlockSpec(memory_space=pltpu.SMEM)] + [whole] * 5,
        out_specs=whole,
        scratch_shapes=[pltpu.VMEM((chips, 2, rows, 256), F32)],
        compiler_params=pltpu.CompilerParams(vmem_limit_bytes=48 * 2**20),
    )(place, q, g, x, mine, peer)


def finished_kernel(place, own_ref, got_ref, q_ref, o_ref, sums_ref):
    raw = own_ref[...] + got_ref[...].astype(F32)
    lane = lax.broadcasted_iota(jnp.int32, (1, 128), 1)
    sums = jnp.zeros((1, 128), F32)
    for n, ref in enumerate((q_ref, o_ref)):
        piece = jnp.concatenate([raw[head, n * 64 : n * 64 + 64] for head in range(2)], axis=1)
        ref[...] = jnp.where(place[2] == 0, piece[:32], piece[32:])
        squares = jnp.sum(jnp.sum(piece * piece, axis=0, keepdims=True), axis=1, keepdims=True)
        sums = sums + jnp.where(lane == place[n], squares, 0.0)
    sums_ref[...] = jnp.broadcast_to(sums[None], sums_ref.shape)


def clip_kernel(place, sums_ref, limits_ref, q_ref, o_ref, grad_q_ref, grad_o_ref):
    total = jnp.sum(sums_ref[...], axis=0)
    every = jnp.minimum(1.0, limits_ref[...] / jnp.sqrt(total / (BLOCK_ROWS * D) + 1e-06))
    lane = lax.broadcasted_iota(jnp.int32, (1, 128), 1)
    for n, (raw_ref, grad_ref) in enumerate(((q_ref, grad_q_ref), (o_ref, grad_o_ref))):
        factor = jnp.sum(jnp.where(lane == place[n], every, 0.0), axis=1, keepdims=True)
        grad_ref[...] = raw_ref[...] * factor


def small_call(kernel, outs, scalars, *arrays):
    whole = pl.BlockSpec(memory_space=pltpu.VMEM)
    return pl.pallas_call(
        kernel,
        out_shape=tuple(jax.ShapeDtypeStruct(shape, F32) for shape in outs),
        in_specs=[pl.BlockSpec(memory_space=pltpu.SMEM)] + [whole] * len(arrays),
        out_specs=(whole,) * len(outs),
    )(scalars, *arrays)


def swap(x, axis):
    return lax.ppermute(x, axis, [(0, 1), (1, 0)])


def spread(x, axes, n):
    return lax.all_to_all(
        jnp.broadcast_to(x[None], (n,) + x.shape), axes, split_axis=0, concat_axis=0, tiled=True
    )


def place_of(y, x, half, core):
    return ((y * 4 + x) * 2 + half) * 2 + core


def lines(first_along_x):
    groups = []
    for half in range(2):
        for core in range(2):
            for n in range(4):
                if (core == 0) == first_along_x:
                    groups.append([place_of(n, m, half, core) for m in range(4)])
                else:
                    groups.append([place_of(m, n, half, core) for m in range(4)])
    return groups


def to_plane(block):
    for along_x in (True, False):
        block = lax.all_to_all(
            jnp.broadcast_to(block[None], (4,) + block.shape),
            CTX,
            split_axis=0,
            concat_axis=0,
            axis_index_groups=lines(along_x),
            tiled=True,
        ).reshape(-1, HD)
    return block.reshape(16, -1, HD)


def shards(layer_input, queries, keys, values, out_weight, out_grad, query_limits, output_limits):
    y, x, half, core, head = (lax.axis_index(a) for a in CTX + ("head",))
    first = core == 0

    n, cols = keys.shape[0], out_weight.shape[1]
    block = jnp.concatenate([keys, values, out_weight.T, queries], axis=0)
    block = jnp.stack([block[:, :HD], block[:, HD:]], axis=0)
    block = lax.all_to_all(block, "core", split_axis=0, concat_axis=0, tiled=True)
    q2 = block[:, 2 * n + cols :].reshape(2 * n, HD)

    mine = block[:, : 2 * n + cols].reshape(2 * (2 * n + cols), HD)
    all_mine = to_plane(mine)
    all_peer = to_plane(lax.optimization_barrier((swap(mine, "zh"), all_mine))[0])

    def both(a):
        other = swap(a, "core")
        return jnp.concatenate([jnp.where(first, a, other), jnp.where(first, other, a)], axis=0)

    g2, x2 = both(out_grad), both(layer_input)
    place = jnp.stack([y * 4 + x, half, core]).astype(jnp.int32)
    parts = attention(place, q2, g2, x2, all_mine, all_peer)

    parts = lax.all_to_all(parts, ("y", "x", "core"), split_axis=0, concat_axis=0, tiled=True)
    summed = jnp.sum(parts.astype(F32).reshape(16, 2, HD, HD), axis=0)
    got = swap(summed.astype(BF), "zh")
    place = jnp.stack([y, 4 + head // 2, half]).astype(jnp.int32)
    shape = (D // 64, 2 * HD)
    raw_q, raw_o, sums = small_call(finished_kernel, (shape, shape, (8, 1, 128)), place, summed, got)

    sums = lax.all_to_all(sums, ("x", "core"), split_axis=0, concat_axis=0, tiled=True)
    sums = spread(jnp.sum(sums, axis=0), ("y", "head"), 32)
    limits = jnp.concatenate([query_limits, output_limits, jnp.ones(120, F32)])[None]
    grad_wq, grad_wo = small_call(clip_kernel, (shape, shape), place, sums, limits, raw_q, raw_o)
    return (grad_wq, grad_wo.T)


def solution(mesh):
    fine = Mesh(mesh.devices.reshape(4, 4, 2, 2, 8), CTX + ("head",))
    in_specs = (
        P(CTX, None),
        P(CTX, "head"),
        P(CTX, "head"),
        P(CTX, "head"),
        P("head", CTX),
        P(CTX, None),
        P(),
        P(),
    )
    out_specs = (P(CTX, "head"), P("head", CTX))
    return jax.shard_map(shards, mesh=fine, in_specs=in_specs, out_specs=out_specs, check_vma=False)
```

```python
import math

import jax
import jax.numpy as jnp
from jax import lax
from jax.experimental import pallas as pl
from jax.experimental.pallas import tpu as pltpu
from jax.sharding import Mesh, PartitionSpec as P

D = 2048
HD = 128
BLOCK_ROWS = 512
SCALE = 1.0 / math.sqrt(HD)
SCALE_LOG2E = SCALE * math.log2(math.e)
CTX = ("y", "x", "zh", "core")
PLANE = ("y", "x")
BF = jnp.bfloat16
F32 = jnp.float32


def dot(left, right, dims):
    return lax.dot_general(left, right, (dims, ((), ())), preferred_element_type=F32)


def fold(x, op):
    return op(x[:, :HD], x[:, HD:])


def attention_kernel(place, q_ref, g_ref, x_ref, mine_ref, peer_ref, part_ref, s_ref):
    last, half, core = place[0], place[1], place[2]
    q = q_ref[...]
    rows = q.shape[0]
    chips = peer_ref.shape[0]
    steps = [(i, t) for i in range(chips) for t in range(2)]
    chip = [jnp.where(core == 0, i, i % 4 * 4 + i // 4) for i in range(chips)]

    sources = (mine_ref, peer_ref)

    def keys(i, t):
        return sources[t][i, 0:256, :]

    def values(i, t):
        return sources[t][i, 256:512, :]

    r = lax.broadcasted_iota(jnp.int32, (rows, 256), 0)
    c = lax.broadcasted_iota(jnp.int32, (rows, 256), 1)
    ahead = [c - r, c - r + (1 - 2 * half) * 256]

    top = jnp.full((rows, HD), -jnp.inf, F32)
    for i, t in steps:
        s = dot(q, keys(i, t), ((1,), (1,)))
        s = jnp.where(ahead[t] <= (last - chip[i]) * 512, s, -jnp.inf)
        s_ref[i, t] = s
        top = jnp.maximum(top, fold(s, jnp.maximum))
    top = jnp.max(top, axis=1, keepdims=True)

    g = jnp.zeros((rows, HD), F32)
    for i in range(chips):
        near, far = mine_ref[i, 512:576, :], peer_ref[i, 512:576, :]
        weight = jnp.concatenate(
            [jnp.where(half == 0, near, far), jnp.where(half == 0, far, near)], axis=0
        )
        g = g + dot(g_ref[:, pl.ds(pl.multiple_of(chip[i] * HD, HD), HD)], weight, ((1,), (0,)))
    g = g.astype(BF)

    total = jnp.zeros((rows, HD), F32)
    out = jnp.zeros((rows, HD), F32)
    for i, t in steps:
        e = jnp.exp2((s_ref[i, t] - top) * SCALE_LOG2E)
        s_ref[i, t] = e
        total = total + fold(e, jnp.add)
        out = out + dot(e.astype(BF), values(i, t), ((1,), (0,)))
    inverse = 1.0 / jnp.sum(total, axis=1, keepdims=True)
    attn = (out * inverse).astype(BF)
    delta = jnp.sum(g.astype(F32) * attn.astype(F32), axis=1, keepdims=True)

    grad = jnp.zeros((rows, HD), F32)
    for i, t in steps:
        dp = dot(g, values(i, t), ((1,), (1,)))
        ds = s_ref[i, t] * (dp - delta)
        grad = grad + dot(ds.astype(BF), keys(i, t), ((1,), (0,)))
    grad = (grad * (inverse * SCALE)).astype(BF)

    for i in range(chips):
        cut = slice(i * HD, (i + 1) * HD)
        for n, (left, right) in enumerate(((x_ref, grad), (g_ref, attn))):
            part = dot(left[:, cut], right, ((0,), (0,))).astype(BF)
            for m in range(4):
                half_of, core_of = m // 2, m % 2
                to = n * 64 + half_of * 32
                part_ref[2 * i + core_of, to : to + 32, :] = part[m * 32 : m * 32 + 32]


def attention(place, q, g, x, mine, peer):
    rows = q.shape[0]
    chips = peer.shape[0]
    whole = pl.BlockSpec(memory_space=pltpu.VMEM)
    return pl.pallas_call(
        attention_kernel,
        out_shape=jax.ShapeDtypeStruct((2 * chips, HD, HD), BF),
        in_specs=[pl.BlockSpec(memory_space=pltpu.SMEM)] + [whole] * 5,
        out_specs=whole,
        scratch_shapes=[pltpu.VMEM((chips, 2, rows, 256), F32)],
        compiler_params=pltpu.CompilerParams(vmem_limit_bytes=48 * 2**20),
    )(place, q, g, x, mine, peer)


def finished_kernel(place, own_ref, got_ref, q_ref, o_ref, sums_ref):
    raw = own_ref[...] + got_ref[...].astype(F32)
    lane = lax.broadcasted_iota(jnp.int32, (1, 128), 1)
    sums = jnp.zeros((1, 128), F32)
    for n, ref in enumerate((q_ref, o_ref)):
        piece = jnp.concatenate([raw[head, n * 64 : n * 64 + 64] for head in range(2)], axis=1)
        ref[...] = jnp.where(place[2] == 0, piece[:32], piece[32:])
        squares = jnp.sum(jnp.sum(piece * piece, axis=0, keepdims=True), axis=1, keepdims=True)
        sums = sums + jnp.where(lane == place[n], squares, 0.0)
    sums_ref[...] = jnp.broadcast_to(sums[None], sums_ref.shape)


def clip_kernel(place, q_limits, o_limits, sums_ref, q_ref, o_ref, grad_q_ref, grad_o_ref):
    total = jnp.sum(sums_ref[...], axis=0)
    lane = lax.broadcasted_iota(jnp.int32, (1, 128), 1)
    gradients = ((q_ref, grad_q_ref, q_limits[place[0]]), (o_ref, grad_o_ref, o_limits[place[1] - 4]))
    for n, (raw_ref, grad_ref, limit) in enumerate(gradients):
        mine = jnp.sum(jnp.where(lane == place[n], total, 0.0), axis=1, keepdims=True)
        spread_of = jnp.sqrt(mine / (BLOCK_ROWS * D) + 1e-06)
        grad_ref[...] = raw_ref[...] * jnp.minimum(1.0, limit / spread_of)


def small_call(kernel, outs, scalars, arrays):
    whole = pl.BlockSpec(memory_space=pltpu.VMEM)
    return pl.pallas_call(
        kernel,
        out_shape=tuple(jax.ShapeDtypeStruct(shape, F32) for shape in outs),
        in_specs=[pl.BlockSpec(memory_space=pltpu.SMEM)] * len(scalars) + [whole] * len(arrays),
        out_specs=(whole,) * len(outs),
    )(*scalars, *arrays)


def swap(x, axis):
    return lax.ppermute(x, axis, [(0, 1), (1, 0)])


def spread(x, axes, n):
    return lax.all_to_all(
        jnp.broadcast_to(x[None], (n,) + x.shape), axes, split_axis=0, concat_axis=0, tiled=True
    )


def place_of(y, x, half, core):
    return ((y * 4 + x) * 2 + half) * 2 + core


def lines(first_along_x):
    groups = []
    for half in range(2):
        for core in range(2):
            for n in range(4):
                if (core == 0) == first_along_x:
                    groups.append([place_of(n, m, half, core) for m in range(4)])
                else:
                    groups.append([place_of(m, n, half, core) for m in range(4)])
    return groups


def to_plane(block):
    for along_x in (True, False):
        block = lax.all_to_all(
            jnp.broadcast_to(block[None], (4,) + block.shape),
            CTX,
            split_axis=0,
            concat_axis=0,
            axis_index_groups=lines(along_x),
            tiled=True,
        ).reshape(-1, HD)
    return block.reshape(16, -1, HD)


def shards(layer_input, queries, keys, values, out_weight, out_grad, query_limits, output_limits):
    y, x, half, core, head = (lax.axis_index(a) for a in CTX + ("head",))
    first = core == 0

    n, cols = keys.shape[0], out_weight.shape[1]
    block = jnp.concatenate([keys, values, out_weight.T, queries], axis=0)
    block = jnp.stack([block[:, :HD], block[:, HD:]], axis=0)
    block = lax.all_to_all(block, "core", split_axis=0, concat_axis=0, tiled=True)
    q2 = block[:, 2 * n + cols :].reshape(2 * n, HD)

    cuts = (0, n, 2 * n, 2 * n + cols)
    mine = jnp.concatenate([block[:, i:j].reshape(-1, HD) for i, j in zip(cuts, cuts[1:])], axis=0)
    all_mine = to_plane(mine)
    all_peer = to_plane(lax.optimization_barrier((swap(mine, "zh"), all_mine))[0])

    def both(a):
        other = swap(a, "core")
        return jnp.concatenate([jnp.where(first, a, other), jnp.where(first, other, a)], axis=0)

    g2, x2 = both(out_grad), both(layer_input)
    place = jnp.stack([y * 4 + x, half, core]).astype(jnp.int32)
    parts = attention(place, q2, g2, x2, all_mine, all_peer)

    parts = lax.all_to_all(parts, ("y", "x", "core"), split_axis=0, concat_axis=0, tiled=True)
    summed = jnp.sum(parts.astype(F32).reshape(16, 2, HD, HD), axis=0)
    got = swap(summed.astype(BF), "zh")
    place = jnp.stack([y, 4 + head // 2, half]).astype(jnp.int32)
    shape = (D // 64, 2 * HD)
    outs = (shape, shape, (8, 1, 128))
    raw_q, raw_o, sums = small_call(finished_kernel, outs, (place,), (summed, got))

    sums = lax.all_to_all(sums, ("x", "core"), split_axis=0, concat_axis=0, tiled=True)
    sums = spread(jnp.sum(sums, axis=0), ("y", "head"), 32)
    scalars = (place, query_limits, output_limits)
    grad_wq, grad_wo = small_call(clip_kernel, (shape, shape), scalars, (sums, raw_q, raw_o))
    return (grad_wq, grad_wo.T)


def solution(mesh):
    fine = Mesh(mesh.devices.reshape(4, 4, 2, 2, 8), CTX + ("head",))
    in_specs = (
        P(CTX, None),
        P(CTX, "head"),
        P(CTX, "head"),
        P(CTX, "head"),
        P("head", CTX),
        P(CTX, None),
        P(),
        P(),
    )
    out_specs = (P(CTX, "head"), P("head", CTX))
    return jax.shard_map(shards, mesh=fine, in_specs=in_specs, out_specs=out_specs, check_vma=False)
```

```python
import math

import jax
import jax.numpy as jnp
from jax import lax
from jax.experimental import pallas as pl
from jax.experimental.pallas import tpu as pltpu
from jax.sharding import Mesh, PartitionSpec as P

D = 2048
HD = 128
BLOCK_ROWS = 512
SCALE = 1.0 / math.sqrt(HD)
SCALE_LOG2E = SCALE * math.log2(math.e)
CTX = ("y", "x", "zh", "core")
PLANE = ("y", "x")
BF = jnp.bfloat16
F32 = jnp.float32


def dot(left, right, dims):
    return lax.dot_general(left, right, (dims, ((), ())), preferred_element_type=F32)


def fold(x, op):
    return op(x[:, :HD], x[:, HD:])


def attention_kernel(place, q_ref, g_ref, x_ref, mine_ref, peer_ref, part_ref, s_ref):
    last, half, core = place[0], place[1], place[2]
    q = q_ref[...]
    rows = q.shape[0]
    chips = peer_ref.shape[0]
    steps = [(i, t) for i in range(chips) for t in range(2)]
    chip = [jnp.where(core == 0, i, i % 4 * 4 + i // 4) for i in range(chips)]

    sources = (mine_ref, peer_ref)

    def keys(i, t):
        return sources[t][i, 0:256, :]

    def values(i, t):
        return sources[t][i, 256:512, :]

    r = lax.broadcasted_iota(jnp.int32, (rows, 256), 0)
    c = lax.broadcasted_iota(jnp.int32, (rows, 256), 1)
    ahead = [c - r, c - r + (1 - 2 * half) * 256]

    top = jnp.full((rows, HD), -jnp.inf, F32)
    for i, t in steps:
        s = dot(q, keys(i, t), ((1,), (1,)))
        s = jnp.where(ahead[t] <= (last - chip[i]) * 512, s, -jnp.inf)
        s_ref[i, t] = s
        top = jnp.maximum(top, fold(s, jnp.maximum))
    top = jnp.max(top, axis=1, keepdims=True)

    g = jnp.zeros((rows, HD), F32)
    for i in range(chips):
        near, far = mine_ref[i, 512:576, :], peer_ref[i, 512:576, :]
        weight = jnp.concatenate(
            [jnp.where(half == 0, near, far), jnp.where(half == 0, far, near)], axis=0
        )
        g = g + dot(g_ref[:, pl.ds(pl.multiple_of(chip[i] * HD, HD), HD)], weight, ((1,), (0,)))
    g = g.astype(BF)

    total = jnp.zeros((rows, HD), F32)
    out = jnp.zeros((rows, HD), F32)
    for i, t in steps:
        e = jnp.exp2((s_ref[i, t] - top) * SCALE_LOG2E)
        s_ref[i, t] = e
        total = total + fold(e, jnp.add)
        out = out + dot(e.astype(BF), values(i, t), ((1,), (0,)))
    inverse = 1.0 / jnp.sum(total, axis=1, keepdims=True)
    attn = (out * inverse).astype(BF)
    delta = jnp.sum(g.astype(F32) * attn.astype(F32), axis=1, keepdims=True)

    grad = jnp.zeros((rows, HD), F32)
    for i, t in steps:
        dp = dot(g, values(i, t), ((1,), (1,)))
        ds = s_ref[i, t] * (dp - delta)
        grad = grad + dot(ds.astype(BF), keys(i, t), ((1,), (0,)))
    grad = (grad * (inverse * SCALE)).astype(BF)

    for i in range(chips):
        cut = slice(i * HD, (i + 1) * HD)
        for n, (left, right) in enumerate(((x_ref, grad), (g_ref, attn))):
            part = dot(left[:, cut], right, ((0,), (0,))).astype(BF)
            for m in range(4):
                half_of, core_of = m // 2, m % 2
                to = n * 64 + half_of * 32
                part_ref[2 * i + core_of, to : to + 32, :] = part[m * 32 : m * 32 + 32]


def attention(place, q, g, x, mine, peer):
    rows = q.shape[0]
    chips = peer.shape[0]
    whole = pl.BlockSpec(memory_space=pltpu.VMEM)
    return pl.pallas_call(
        attention_kernel,
        out_shape=jax.ShapeDtypeStruct((2 * chips, HD, HD), BF),
        in_specs=[pl.BlockSpec(memory_space=pltpu.SMEM)] + [whole] * 5,
        out_specs=whole,
        scratch_shapes=[pltpu.VMEM((chips, 2, rows, 256), F32)],
        compiler_params=pltpu.CompilerParams(vmem_limit_bytes=48 * 2**20),
    )(place, q, g, x, mine, peer)


def finished_kernel(place, own_ref, got_ref, q_ref, o_ref, sums_ref):
    raw = own_ref[...] + got_ref[...].astype(F32)
    lane = lax.broadcasted_iota(jnp.int32, (1, 128), 1)
    sums = jnp.zeros((1, 128), F32)
    for n, ref in enumerate((q_ref, o_ref)):
        piece = jnp.concatenate([raw[head, n * 64 : n * 64 + 64] for head in range(2)], axis=1)
        ref[...] = jnp.where(place[2] == 0, piece[:32], piece[32:])
        squares = jnp.sum(jnp.sum(piece * piece, axis=0, keepdims=True), axis=1, keepdims=True)
        sums = sums + jnp.where(lane == place[n], squares, 0.0)
    sums_ref[...] = jnp.broadcast_to(sums[None], sums_ref.shape)


def clip_kernel(place, q_limits, o_limits, sums_ref, q_ref, o_ref, grad_q_ref, grad_o_ref):
    total = jnp.sum(sums_ref[...], axis=0)
    lane = lax.broadcasted_iota(jnp.int32, (1, 128), 1)
    gradients = ((q_ref, grad_q_ref, q_limits[place[0]]), (o_ref, grad_o_ref, o_limits[place[1] - 4]))
    for n, (raw_ref, grad_ref, limit) in enumerate(gradients):
        mine = jnp.sum(jnp.where(lane == place[n], total, 0.0), axis=1, keepdims=True)
        spread_of = jnp.sqrt(mine / (BLOCK_ROWS * D) + 1e-06)
        grad_ref[...] = raw_ref[...] * jnp.minimum(1.0, limit / spread_of)


def small_call(kernel, outs, scalars, arrays):
    whole = pl.BlockSpec(memory_space=pltpu.VMEM)
    return pl.pallas_call(
        kernel,
        out_shape=tuple(jax.ShapeDtypeStruct(shape, F32) for shape in outs),
        in_specs=[pl.BlockSpec(memory_space=pltpu.SMEM)] * len(scalars) + [whole] * len(arrays),
        out_specs=(whole,) * len(outs),
    )(*scalars, *arrays)


def swap(x, axis):
    return lax.ppermute(x, axis, [(0, 1), (1, 0)])


def spread(x, axes, n):
    return lax.all_to_all(
        jnp.broadcast_to(x[None], (n,) + x.shape), axes, split_axis=0, concat_axis=0, tiled=True
    )


def place_of(y, x, half, core):
    return ((y * 4 + x) * 2 + half) * 2 + core


def lines(first_along_x):
    groups = []
    for half in range(2):
        for core in range(2):
            for n in range(4):
                if (core == 0) == first_along_x:
                    groups.append([place_of(n, m, half, core) for m in range(4)])
                else:
                    groups.append([place_of(m, n, half, core) for m in range(4)])
    return groups


def to_plane(block):
    for along_x in (True, False):
        block = lax.all_to_all(
            jnp.broadcast_to(block[None], (4,) + block.shape),
            CTX,
            split_axis=0,
            concat_axis=0,
            axis_index_groups=lines(along_x),
            tiled=True,
        ).reshape(-1, HD)
    return block.reshape(16, -1, HD)


def shards(layer_input, queries, keys, values, out_weight, out_grad, query_limits, output_limits):
    y, x, half, core, head = (lax.axis_index(a) for a in CTX + ("head",))
    first = core == 0

    n, cols = keys.shape[0], out_weight.shape[1]
    block = jnp.concatenate([keys, values, out_weight.T, queries], axis=0)
    block = jnp.stack([block[:, :HD], block[:, HD:]], axis=0)
    block = lax.all_to_all(block, "core", split_axis=0, concat_axis=0, tiled=True)
    q2 = block[:, 2 * n + cols :].reshape(2 * n, HD)

    cuts = (0, n, 2 * n, 2 * n + cols)
    mine = jnp.concatenate([block[:, i:j].reshape(-1, HD) for i, j in zip(cuts, cuts[1:])], axis=0)
    all_mine = to_plane(mine)
    def both(a):
        other = swap(a, "core")
        return jnp.concatenate([jnp.where(first, a, other), jnp.where(first, other, a)], axis=0)

    ready = (swap(mine, "zh"), all_mine, both(out_grad), both(layer_input))
    peer, all_mine, g2, x2 = lax.optimization_barrier(ready)
    all_peer = to_plane(peer)

    place = jnp.stack([y * 4 + x, half, core]).astype(jnp.int32)
    parts = attention(place, q2, g2, x2, all_mine, all_peer)

    parts = lax.all_to_all(parts, ("y", "x", "core"), split_axis=0, concat_axis=0, tiled=True)
    summed = jnp.sum(parts.astype(F32).reshape(16, 2, HD, HD), axis=0)
    got = swap(summed.astype(BF), "zh")
    place = jnp.stack([y, 4 + head // 2, half]).astype(jnp.int32)
    shape = (D // 64, 2 * HD)
    outs = (shape, shape, (8, 1, 128))
    raw_q, raw_o, sums = small_call(finished_kernel, outs, (place,), (summed, got))

    sums = lax.all_to_all(sums, ("x", "core"), split_axis=0, concat_axis=0, tiled=True)
    sums = spread(jnp.sum(sums, axis=0), ("y", "head"), 32)
    scalars = (place, query_limits, output_limits)
    grad_wq, grad_wo = small_call(clip_kernel, (shape, shape), scalars, (sums, raw_q, raw_o))
    return (grad_wq, grad_wo.T)


def solution(mesh):
    fine = Mesh(mesh.devices.reshape(4, 4, 2, 2, 8), CTX + ("head",))
    in_specs = (
        P(CTX, None),
        P(CTX, "head"),
        P(CTX, "head"),
        P(CTX, "head"),
        P("head", CTX),
        P(CTX, None),
        P(),
        P(),
    )
    out_specs = (P(CTX, "head"), P("head", CTX))
    return jax.shard_map(shards, mesh=fine, in_specs=in_specs, out_specs=out_specs, check_vma=False)
```
